32 devices in a mesh: poles: 2 (over y), row: 8 (over z, x), col: 2 (over core).
Axes of the slice: x: 2, y: 2, z: 4, core: 2. Of those that a mesh axis runs over, the one named last changes fastest.
Arguments:
- ainv_top: bfloat16 [2048, 1024], P(('poles', 'row', 'col')), parts along dimension 0, as said below
- l_parent: bfloat16 [16, 1024, 512], P(('poles', 'row'), None, 'col'), parts along dimension 0, may hold values from -0.25 to 0.25
- dinv_parent: bfloat16 [16, 512, 512], P(('poles', 'row'), None, 'col'), parts along dimension 0, as said below
- keep_parent: int32 [16, 2], P(('poles', 'row')), parts along dimension 0, may hold values from 0 to 1
- l_child: bfloat16 [32, 1536, 512], P(('poles', 'row'), None, 'col'), parts along dimension 0, may hold values from -0.25 to 0.25
- dinv_child: bfloat16 [32, 512, 512], P(('poles', 'row'), None, 'col'), parts along dimension 0, as said below
- keep_child: int32 [32, 2], P(('poles', 'row')), parts along dimension 0, may hold values from 0 to 1, as said below
- parent_of: int32 [32], P(('poles', 'row')), parts along dimension 0, may hold values from 0 to 7, as said below
Outputs:
- parent_diag: bfloat16 [16, 512, 512], P(('poles', 'row'), None, 'col'), parts along dimension 0
- child_column: bfloat16 [32, 1536, 512], P(('poles', 'row'), None, 'col'), parts along dimension 0
- child_diag: bfloat16 [32, 512, 512], P(('poles', 'row'), None, 'col'), parts along dimension 0
The draws below stay inside these ranges and needn't reach their ends.
There are 2 independent parts, one for each index of `poles`. The reference program is written for one: setup_inputs(seed, part) draws one part's arguments, and reference() takes and returns one part's arrays. A program takes and returns all parts, laid end to end along the dimension named above; each array names one. Nothing has to cross between parts.
Inputs may be any that keep to these rules, and one draw needn't show every extreme that they name: `ainv_top`: symmetric. `dinv_parent`: each block symmetric. `dinv_child`: each block symmetric. `keep_child`: a lower-level supernode keeps a top block only where its parent keeps it. `parent_of`: the parent of a supernode held by row index r is upper-level supernode number r + d with |d| <= 1; the first supernode of each row index has |d| = 1 wherever r + d stays in range.
All inputs are finite; a program needn't handle non-finite values.
Results may differ from the reference program's by a relative error of at most 0.0051.
Values may be sent and summed in bfloat16 or wider, within the bound.
No kernel may reach another device: no remote copies, remote signals or barrier semaphores. Data moves between devices by JAX's collectives and lax.ppermute only.
A program may use at most 64 MiB of HBM per device.

```python
import math
import jax
import jax.numpy as jnp
from jax import lax

B = 512
TOP = 2
HOP = 1
CH_DEV = 2
NP = 8
NC = 16


def symmetric_blocks(key, count, order, strength):
    keys = jax.random.split(key, 4)
    normal_part = jax.random.normal(keys[0], (count, order, order), jnp.float32)
    noise = normal_part
    paired = (noise + jnp.swapaxes(noise, 1, 2)) * (strength / math.sqrt(2.0 * order))
    diagonal = jax.random.uniform(keys[3], (count, order), jnp.float32, 0.7, 1.3)
    block = paired + jnp.eye(order, dtype=jnp.float32)[None, :, :] * diagonal[:, None, :]
    return block


def tree_draw(key):
    keys = jax.random.split(key, 4)
    slots = jnp.arange(NC, dtype=jnp.int32)
    owner = slots // CH_DEV
    offset = jax.random.randint(keys[0], (NC,), -HOP, HOP + 1, jnp.int32)
    signs = 2 * jax.random.randint(keys[1], (NC,), 0, 2, jnp.int32) - 1
    offset = jnp.where(slots % CH_DEV == 0, signs * HOP, offset)
    parent = jnp.clip(owner + offset, 0, NP - 1).astype(jnp.int32)
    keep_upper = (jax.random.randint(keys[2], (NP, TOP), 0, 4, jnp.int32) > 0).astype(jnp.int32)
    keep_lower = (jax.random.randint(keys[3], (NC, TOP), 0, 4, jnp.int32) > 0).astype(jnp.int32) * keep_upper[parent]
    return (parent, keep_upper, keep_lower)


def draw_parent_of(key, part):
    return tree_draw(key)[0]


def draw_keep_parent(key, part):
    return tree_draw(key)[1]


def draw_keep_child(key, part):
    return tree_draw(key)[2]


def draw_ainv_top(key, part):
    key = jax.random.fold_in(key, 11)
    return symmetric_blocks(key, 1, TOP * B, 0.4)[0].astype(jnp.bfloat16)


def draw_dinv_parent(key, part):
    key = jax.random.fold_in(key, 12)
    return symmetric_blocks(key, NP, B, 0.3).astype(jnp.bfloat16)


def draw_dinv_child(key, part):
    key = jax.random.fold_in(key, 13)
    return symmetric_blocks(key, NC, B, 0.3).astype(jnp.bfloat16)


def block_scale(own_key, dims, pieces, least, high):
    gain, own = 1.0, jax.random.fold_in(own_key, 6)
    for axis_at, shards_of in pieces:
        steps = jnp.exp(jax.random.uniform(jax.random.fold_in(own, axis_at), (shards_of,), jnp.float32, least / len(pieces), high / len(pieces)))
        gain = gain * jnp.repeat(steps, dims[axis_at] // shards_of).reshape([-1 if axis == axis_at else 1 for axis in range(len(dims))])
    return gain


def normal_values(stream_key, shape, scale, bound, shards=(), kind=jnp.bfloat16):
    result = jax.random.normal(stream_key, shape, jnp.float32) * scale
    if len(shards) > 0:
        result = block_scale(stream_key, shape, shards, -0.22, 0.18) * result
    return jnp.clip(result, min=-bound, max=bound).astype(kind)


def setup_inputs(seed: int = 0, part: int = 0) -> dict:
    splits = jax.random.split(jax.random.key(seed), 9)
    part_splits = jax.random.split(jax.random.fold_in(splits[8], part), 9)
    return {
        "ainv_top": draw_ainv_top(jax.random.fold_in(jax.random.fold_in(splits[8], part), 71), part),
        "l_parent": normal_values(part_splits[1], (NP, TOP * B, B), B ** -0.5, 0.25, ((0, 8), (2, 2))),
        "dinv_parent": draw_dinv_parent(jax.random.fold_in(jax.random.fold_in(splits[8], part), 71), part),
        "keep_parent": draw_keep_parent(jax.random.fold_in(jax.random.fold_in(splits[8], part), 71), part),
        "l_child": normal_values(part_splits[4], (NC, (1 + TOP) * B, B), B ** -0.5, 0.25, ((0, 8), (2, 2))),
        "dinv_child": draw_dinv_child(jax.random.fold_in(jax.random.fold_in(splits[8], part), 71), part),
        "keep_child": draw_keep_child(jax.random.fold_in(jax.random.fold_in(splits[8], part), 71), part),
        "parent_of": draw_parent_of(jax.random.fold_in(jax.random.fold_in(splits[8], part), 71), part),
    }


def reference(ainv_top, l_parent, dinv_parent, keep_parent, l_child, dinv_child, keep_child, parent_of):
    parent_rows = jnp.repeat(keep_parent, B, axis=1).astype(jnp.bfloat16)
    x_parent = l_parent * parent_rows[:, :, None]
    top_parent = jnp.einsum("ij,pjc->pic", ainv_top.astype(jnp.float32), x_parent.astype(jnp.float32))
    g_parent = (-top_parent).astype(jnp.bfloat16)
    parent_diag = (dinv_parent.astype(jnp.float32) - jnp.einsum("pic,pid->pcd", x_parent.astype(jnp.float32), g_parent.astype(jnp.float32))).astype(jnp.bfloat16)
    column = jnp.concatenate([parent_diag, g_parent], axis=1)
    child_rows = jnp.concatenate([jnp.ones((NC, B), jnp.int32), jnp.repeat(keep_child, B, axis=1)], axis=1).astype(jnp.bfloat16)
    x_child = l_child * child_rows[:, :, None]

    def one_child(items):
        panel, dinv_block, mask_rows, parent = items
        chosen = column[parent]
        own = panel[:B]
        upper_rows = panel[B:]
        product = jnp.dot(chosen, own, preferred_element_type=jnp.float32)
        upper = jnp.dot(chosen[B:].T, upper_rows, preferred_element_type=jnp.float32)
        lower = jnp.dot(ainv_top, upper_rows, preferred_element_type=jnp.float32)
        product = product + jnp.concatenate([upper, lower], axis=0)
        g_child = (-(product * mask_rows.astype(jnp.float32)[:, None])).astype(jnp.bfloat16)
        diag = (dinv_block.astype(jnp.float32) - jnp.dot(panel.T, g_child, preferred_element_type=jnp.float32)).astype(jnp.bfloat16)
        return g_child, diag

    child_column, child_diag = lax.map(one_child, (x_child, dinv_child, child_rows, parent_of.astype(jnp.int32)))
    return parent_diag, child_column, child_diag
```

```python
import functools

import jax
import jax.numpy as jnp
from jax import lax
from jax.experimental import pallas as pl
from jax.experimental.pallas import tpu as pltpu
from jax.sharding import PartitionSpec as P

DIRECT = 4
F32 = jnp.float32
BF16 = jnp.bfloat16


def dot(a, b):
    return jnp.dot(a, b, preferred_element_type=F32)


def dot_t(a, b):
    return lax.dot_general(a, b, (((0,), (0,)), ((), ())), preferred_element_type=F32)


def kernel(
    place_ref,
    slot_ref,
    keep_ref,
    *refs,
    pieces,
):
    n_a = len(pieces)
    a_refs, refs = refs[:n_a], refs[n_a:]
    (
        xp, xp_o, xs, xs_o, xf, xf_o,
        dp, dp_o, ds, ds_o, df, df_o,
        lc, lc_o, dc,
        pd_out, cc_out, cd_out,
        a, x, d, c, dcv, g, v, t, pd, cc, cd,
        sem, out_sem,
    ) = refs
    half = lc.shape[-1]
    width = 2 * half
    tops = xp.shape[0]
    me = place_ref[0]
    mine = pl.multiple_of(me * half, half)
    other = pl.multiple_of((1 - me) * half, half)
    copies = []

    def start(src, dst):
        copy = pltpu.make_async_copy(src, dst, sem.at[len(copies)])
        copy.start()
        copies.append(copy)

    def start_rows(src, dst):
        start(src.at[pl.ds(mine, half)], dst.at[pl.ds(0, half)])
        start(src.at[pl.ds(other, half)], dst.at[pl.ds(half, half)])

    cols = (pl.ds(0, half), pl.ds(half, half))
    for slot, (left, right) in enumerate(((xp, xp_o), (xs, xs_o), (xf, xf_o))):
        start(left, x.at[slot, :, cols[0]])
        start(right, x.at[slot, :, cols[1]])
    for k in range(lc.shape[0]):
        for side, src in enumerate((lc, lc_o)):
            start_rows(src.at[k], c.at[k, side])
            start(src.at[k, pl.ds(width, tops)], c.at[k, side, pl.ds(width, tops)])
    for ref, piece in zip(a_refs, pieces):
        if piece is None:
            start(ref, a)
            continue
        planes = ref.shape[0]
        block = ref.shape[1]
        flip_pair, flip_core = piece
        pair = 1 - place_ref[2] if flip_pair else place_ref[2]
        core = 1 - me if flip_core else me
        for k in range(planes):
            plane = lax.rem(place_ref[1] + planes - k, planes)
            row = pl.multiple_of(((plane * 2 + pair) * 2 + core) * block, block)
            start(ref.at[k], a.at[pl.ds(row, block)])
    for slot, (left, right) in enumerate(((dp, dp_o), (ds, ds_o), (df, df_o))):
        start_rows(left, d.at[slot, :, cols[0]])
        start_rows(right, d.at[slot, :, cols[1]])
    for k in range(lc.shape[0]):
        start_rows(dc.at[k], dcv.at[k])
    for copy in copies:
        copy.wait()

    step = half
    for i in range(tops // step):
        rows = pl.ds(i * step, step)
        g[rows, :] = (-dot(a[rows, :], x[0, :, :half])).astype(BF16)
    for i in range(2):
        rows = pl.ds(i * half, half)
        pd[rows, :] = (
            d[0, rows, :half].astype(F32) - dot_t(x[0, :, rows], g[...])
        ).astype(BF16)
    outs = []

    def finish(src, dst):
        copy = pltpu.make_async_copy(src, dst, out_sem.at[len(outs)])
        copy.start()
        outs.append(copy)

    def finish_rows(src, dst):
        finish(src.at[pl.ds(0, half)], dst.at[pl.ds(mine, half)])
        finish(src.at[pl.ds(half, half)], dst.at[pl.ds(other, half)])

    finish_rows(pd, pd_out)

    for k in range(lc.shape[0]):
        slot = slot_ref[k]
        u = c[k, 0, pl.ds(0, width), :]
        for i in range(tops // step):
            rows = pl.ds(i * step, step)
            kept = keep_ref[k, i * step // width] > 0
            w = c[k, 0, pl.ds(width + i * step, step), :].astype(F32)
            v[rows, :] = (
                dot(x[slot, rows, :], u) - jnp.where(kept, w, 0.0)
            ).astype(BF16)
        for i in range(tops // step):
            rows = pl.ds(i * step, step)
            kept = keep_ref[k, i * step // width] > 0
            tile = dot(a[rows, :], v[...]).astype(BF16)
            t[rows, :] = tile
            cc[k, pl.ds(width + i * step, step), :] = jnp.where(kept, tile, jnp.zeros_like(tile))
        for i in range(2):
            rows = pl.ds(i * half, half)
            y = dot(d[slot, rows, :], u) + dot_t(x[slot, :, rows], t[...])
            cc[k, rows, :] = (-y).astype(BF16)
        finish_rows(cc.at[k], cc_out.at[k])
        finish(cc.at[k, pl.ds(width, tops)], cc_out.at[k, pl.ds(width, tops)])
        for side in range(2):
            rows = pl.ds(side * half, half)
            cd[k, rows, :] = (
                dcv[k, rows, :].astype(F32) - dot_t(c[k, side], cc[k])
            ).astype(BF16)
        finish_rows(cd.at[k], cd_out.at[k])
    for copy in outs:
        copy.wait()


def local(ainv_top, l_parent, dinv_parent, keep_parent, l_child, dinv_child, keep_child, parent_of):
    devices = lax.axis_size("row")
    planes = devices // 2
    row = lax.axis_index("row")
    swap = [(i, i ^ 1) for i in range(devices)]
    onward = [(i, i - 2 if i % 2 else i + 2) for i in range(devices)]
    onward = [(i, j) for i, j in onward if 0 <= j < devices]
    cores = [(0, 1), (1, 0)]

    def swapped(x):
        return lax.ppermute(x, "row", swap)

    def crossed(x):
        return lax.ppermute(x, "col", cores)

    half = l_parent.shape[2]
    width = 2 * half
    tops = l_parent.shape[1]
    children = l_child.shape[0]
    rows = jnp.repeat(keep_parent[0], width).astype(BF16)
    xp = l_parent[0] * rows[:, None]
    dp = dinv_parent[0]
    xs = swapped(xp)
    if planes <= DIRECT:
        arrived = [ainv_top]
        for k in range(1, planes):
            arrived.append(
                lax.ppermute(ainv_top, "row", [(i, (i + 2 * k) % devices) for i in range(devices)])
            )
        near = jnp.stack(arrived)
        far = swapped(near)
        a_parts = [near, crossed(near), far, crossed(far)]
        pieces = [(False, False), (False, True), (True, False), (True, True)]
    else:
        a_parts = [lax.all_gather(ainv_top, ("row", "col"), axis=0, tiled=True)]
        pieces = [None]
    ds = swapped(dp)
    xf = lax.ppermute(xs, "row", onward)
    df = lax.ppermute(ds, "row", onward)
    operands = [
        xp, crossed(xp), xs, crossed(xs), xf, crossed(xf),
        dp, crossed(dp), ds, crossed(ds), df, crossed(df),
        l_child, crossed(l_child), dinv_child,
    ]
    place = jnp.stack([lax.axis_index("col"), row // 2, row % 2]).astype(jnp.int32)
    slot = jnp.where(parent_of == row, 0, jnp.where(parent_of == row ^ 1, 1, 2)).astype(jnp.int32)
    smem = pl.BlockSpec(memory_space=pltpu.SMEM)
    hbm = pl.BlockSpec(memory_space=pl.ANY)
    parent_diag, child_column, child_diag = pl.pallas_call(
        functools.partial(kernel, pieces=pieces),
        out_shape=(
            jax.ShapeDtypeStruct((width, half), BF16),
            jax.ShapeDtypeStruct(l_child.shape, BF16),
            jax.ShapeDtypeStruct(dinv_child.shape, BF16),
        ),
        in_specs=[smem] * 3 + [hbm] * (len(a_parts) + len(operands)),
        out_specs=(hbm,) * 3,
        scratch_shapes=[
            pltpu.VMEM((tops, tops), BF16),
            pltpu.VMEM((3, tops, width), BF16),
            pltpu.VMEM((3, width, width), BF16),
            pltpu.VMEM((children, 2, width + tops, half), BF16),
            pltpu.VMEM((children, width, half), BF16),
            pltpu.VMEM((tops, half), BF16),
            pltpu.VMEM((tops, half), BF16),
            pltpu.VMEM((tops, half), BF16),
            pltpu.VMEM((width, half), BF16),
            pltpu.VMEM((children, width + tops, half), BF16),
            pltpu.VMEM((children, width, half), BF16),
            pltpu.SemaphoreType.DMA((64,)),
            pltpu.SemaphoreType.DMA((16,)),
        ],
        compiler_params=pltpu.CompilerParams(vmem_limit_bytes=32 << 20),
    )(place, slot, keep_child, *a_parts, *operands)
    return parent_diag[None], child_column, child_diag


def solution(mesh):
    blocks = P(("poles", "row"), None, "col")
    placed = (
        P(("poles", "row", "col"), None),
        blocks,
        blocks,
        P(("poles", "row"), None),
        blocks,
        blocks,
        P(("poles", "row"), None),
        P(("poles", "row")),
    )
    return jax.shard_map(
        local, mesh=mesh, in_specs=placed, out_specs=(blocks,) * 3, check_vma=False
    )
```

```python
import jax
import jax.numpy as jnp
from jax import lax
from jax.experimental import pallas as pl
from jax.experimental.pallas import tpu as pltpu
from jax.sharding import PartitionSpec as P

DIRECT = 4
F32 = jnp.float32
BF16 = jnp.bfloat16
SEQUENCES = (
    (1, (
        "swapped 0",
        "swapped 1",
    )),
    (1, (
        "swapped 0",
        "far",
    )),
    (1, (
        "swapped 0",
        "a 2",
    )),
)


def dot(a, b):
    return jnp.dot(a, b, preferred_element_type=F32)


def dot_t(a, b):
    return lax.dot_general(a, b, (((0,), (0,)), ((), ())), preferred_element_type=F32)


class Loads:
    def __init__(self, sem):
        self.sem, self.used = sem, 0

    def start(self, src, dst):
        copy = pltpu.make_async_copy(src, dst, self.sem.at[self.used])
        self.used += 1
        copy.start()
        return copy

    def choose(self, which, srcs, dst):
        sem = self.sem.at[self.used]
        self.used += 1
        for k, src in enumerate(srcs):

            @pl.when(which == k)
            def _(src=src):
                pltpu.make_async_copy(src, dst, sem).start()

        return pltpu.make_async_copy(srcs[0], dst, sem)


def wait(copies):
    for copy in copies:
        copy.wait()


def pack_kernel(keep_ref, factor, inverse, *refs):
    parts, whole, sem = refs[:-2], refs[-2], refs[-1]
    width = inverse.shape[0]
    share = width // len(parts)
    loads = Loads(sem)
    copies = [
        (
            loads.start(factor.at[pl.ds(i * width, width)], part.at[pl.ds(0, width)]),
            loads.start(inverse.at[pl.ds(i * share, share)], part.at[pl.ds(width, share)]),
        )
        for i, part in enumerate(parts)
    ]
    for i, part in enumerate(parts):
        wait(copies[i])

        @pl.when(keep_ref[0, i] == 0)
        def _(part=part):
            part[pl.ds(0, width), :] = jnp.zeros((width, part.shape[1]), part.dtype)

        whole[i] = part[...]


def copy_top(place_ref, near, near_o, far, far_o, a):
    planes, block = near.shape[:2]
    span = 2 * block
    me, pair = place_ref[0], place_ref[2]
    for k in range(planes):
        plane = lax.rem(place_ref[1] + planes - k, planes)
        for ref, core in ((near, me), (near_o, 1 - me)):
            row = pl.multiple_of(((plane * 2 + pair) * 2 + core) * block, block)
            a[pl.ds(row, block), :] = ref[k]
        for ref, core in ((far, me), (far_o, 1 - me)):
            row = pl.multiple_of(((plane * 2 + 1 - pair) * 2 + core) * block, block)
            for j in range(planes):
                col = pl.multiple_of((2 * j + 1 - pair) * span, span)
                a[pl.ds(row, block), pl.ds(col, span)] = ref[k, :, j * span : (j + 1) * span]
    for i in range(planes):
        for j in range(planes):
            mine = pl.multiple_of((2 * i + pair) * span, span)
            theirs = pl.multiple_of((2 * j + 1 - pair) * span, span)
            a[pl.ds(theirs, span), pl.ds(mine, span)] = a[pl.ds(mine, span), pl.ds(theirs, span)].T


def sides_of(place_ref, half):
    mine = pl.multiple_of(place_ref[0] * half, half)
    other = pl.multiple_of((1 - place_ref[0]) * half, half)
    return pl.ds(mine, half), pl.ds(other, half)


def parent_kernel(place_ref, *refs):
    own, own_o, dp, pd, a, g = refs[-6:]
    width, half = dp.shape
    parts = own.shape[0]
    if len(refs) == 10:
        copy_top(place_ref, *refs[:4], a)
    else:
        a[...] = refs[0][...]
    head = pl.ds(0, width)
    total = dot(a[:, :width], own[0, head, :])
    for j in range(1, parts):
        total += dot(a[:, j * width : (j + 1) * width], own[j, head, :])
    g[...] = total.astype(BF16)
    for r, at in zip((own, own_o), sides_of(place_ref, half)):
        y = dp[at, :].astype(F32)
        for j in range(parts):
            y += dot_t(r[j, head, :], g[j * width : (j + 1) * width, :])
        pd[at, :] = y.astype(BF16)


def child_kernel(place_ref, slot_ref, keep_ref, a, lc, lc_o, dc, own, own_o, *refs):
    parts = own.shape[0]
    swapped, beyond, refs = refs[:parts], refs[parts : 2 * parts], refs[2 * parts :]
    swapped_o, beyond_o, cc_out, cd_out, x, v, t, cc, cd, sem = refs
    children, _, half = lc.shape
    width = 2 * half
    tops = a.shape[0]
    head, below, tail = pl.ds(0, width), pl.ds(width, tops), pl.ds(width, half)
    ends = sides_of(place_ref, half)
    holds = (place_ref[0], 1 - place_ref[0])
    loads = Loads(sem)
    chosen, outs = [], []
    for k in range(children):
        chosen.append([])
        for j in range(parts):
            for i, srcs in enumerate(
                (
                    (own.at[j], swapped[j], beyond[j]),
                    (own_o.at[j], swapped_o.at[j], beyond_o.at[j]),
                )
            ):
                chosen[k].append(loads.choose(slot_ref[k], srcs, x.at[k, i, j]))
    for k in range(children):
        wait(chosen[k])
        for j in range(parts):
            rows = pl.ds(j * width, width)
            w = lc[k, pl.ds(width + j * width, width), :].astype(F32)
            part = dot(x[k, 0, j, head, :], lc[k, ends[0], :])
            part += dot(x[k, 1, j, head, :], lc[k, ends[1], :])
            v[k, rows, :] = (part - jnp.where(keep_ref[k, j] > 0, w, 0.0)).astype(BF16)
    for k in range(children):
        t[k] = dot(a[...], v[k]).astype(BF16)
    for k in range(children):
        for i in range(2):
            y = dot(x[k, 0, holds[i], tail, :], lc[k, ends[0], :])
            y += dot(x[k, 1, holds[i], tail, :], lc[k, ends[1], :])
            for j in range(parts):
                y += dot_t(x[k, i, j, head, :], t[k, j * width : (j + 1) * width, :])
            cc[k, ends[i], :] = (-y).astype(BF16)
        outs.append(loads.start(cc.at[k], cc_out.at[k, head]))
        for j in range(parts):

            @pl.when(keep_ref[k, j] == 0)
            def _(k=k, j=j):
                t[k, pl.ds(j * width, width), :] = jnp.zeros((width, half), BF16)

        outs.append(loads.start(t.at[k], cc_out.at[k, below]))
    for k in range(children):
        for i, r in enumerate((lc, lc_o)):
            y = dot_t(r[k, below, :], t[k]) + dot_t(r[k, head, :], cc[k])
            cd[k, ends[i], :] = (dc[k, ends[i], :].astype(F32) - y).astype(BF16)
        outs.append(loads.start(cd.at[k], cd_out.at[k]))
    wait(outs)


def local(ainv_top, l_parent, dinv_parent, keep_parent, l_child, dinv_child, keep_child, parent_of):
    devices = lax.axis_size("row")
    planes = devices // 2
    row = lax.axis_index("row")
    swap = [(i, i ^ 1) for i in range(devices)]
    onward = [(i, i - 2 if i % 2 else i + 2) for i in range(devices)]
    onward = [(i, j) for i, j in onward if 0 <= j < devices]
    cores = [(0, 1), (1, 0)]
    half = l_parent.shape[2]
    width = 2 * half
    tops = l_parent.shape[1]
    parts = tops // width
    rows = width + width // parts
    children = l_child.shape[0]
    direct = planes <= DIRECT
    smem = pl.BlockSpec(memory_space=pltpu.SMEM)
    vmem = pl.BlockSpec(memory_space=pltpu.VMEM)
    hbm = pl.BlockSpec(memory_space=pl.ANY)
    packed = jax.ShapeDtypeStruct((rows, half), BF16)
    *own, whole = pl.pallas_call(
        pack_kernel,
        out_shape=(packed,) * parts + (jax.ShapeDtypeStruct((parts, rows, half), BF16),),
        in_specs=[smem] + [hbm] * 2,
        out_specs=(vmem,) * (parts + 1),
        scratch_shapes=[pltpu.SemaphoreType.DMA((2 * parts,))],
        compiler_params=pltpu.CompilerParams(vmem_limit_bytes=60 << 20),
    )(keep_parent, l_parent[0], dinv_parent[0])
    ainv_top, *own = lax.optimization_barrier((ainv_top, *own))
    got = {"own": whole, "c": l_child, "a": ainv_top}
    got.update((f"own {j}", own[j]) for j in range(parts))

    moves = {}
    for j in range(parts):
        moves[f"swapped {j}"] = (f"own {j}", "row", swap)
        moves[f"beyond {j}"] = (f"swapped {j}", "row", onward)
    for name in ("own", "c", "swapped", "beyond"):
        moves[name + " other"] = (name, "col", cores)
    if direct:
        for k in range(1, planes):
            moves[f"a {k}"] = ("a", "row", [(i, (i + 2 * k) % devices) for i in range(devices)])
        moves["far"] = ("sides", "row", swap)
        moves["near other"] = ("near", "col", cores)
        moves["far other"] = ("far", "col", cores)

    def value(name):
        if name in got:
            return got[name]
        if name in ("swapped", "beyond"):
            got[name] = jnp.stack([value(f"{name} {j}") for j in range(parts)])
        elif name in ("near", "sides"):
            near = jnp.stack([got["a"], *(value(f"a {k}") for k in range(1, planes))])
            sides = near.reshape(planes, near.shape[1], planes, 2, -1)
            sides = jnp.where(row % 2 == 0, sides[:, :, :, 0], sides[:, :, :, 1])
            got["near"] = near
            got["sides"] = sides.reshape(planes, near.shape[1], -1)
        else:
            source, axis, pairs = moves[name]
            got[name] = lax.ppermute(value(source), axis, pairs)
        return got[name]

    for window, sequence in SEQUENCES:
        sequence = [name for name in sequence if name in moves]
        for i, name in enumerate(sequence):
            if name in got:
                continue
            source, axis, pairs = moves[name]
            sent = value(source)
            if i >= window:
                sent = lax.optimization_barrier((sent, value(sequence[i - window])))[0]
            got[name] = lax.ppermute(sent, axis, pairs)
    if direct:
        top = [value(name) for name in ("near", "near other", "far", "far other")]
    else:
        top = [lax.all_gather(ainv_top, ("row", "col"), axis=0, tiled=True)]
    place = jnp.stack([lax.axis_index("col"), row // 2, row % 2]).astype(jnp.int32)
    slot = jnp.where(parent_of == row, 0, jnp.where(parent_of == row ^ 1, 1, 2)).astype(jnp.int32)
    parent_diag, full = pl.pallas_call(
        parent_kernel,
        out_shape=(
            jax.ShapeDtypeStruct((width, half), BF16),
            jax.ShapeDtypeStruct((tops, tops), BF16),
        ),
        in_specs=[smem] + [vmem] * (len(top) + 3),
        out_specs=(vmem,) * 2,
        scratch_shapes=[pltpu.VMEM((tops, half), BF16)],
        compiler_params=pltpu.CompilerParams(vmem_limit_bytes=12 << 20),
        cost_estimate=pl.CostEstimate(
            flops=2 * tops * half * (tops + width), bytes_accessed=1 << 20, transcendentals=0
        ),
    )(place, *top, whole, value("own other"), dinv_parent[0])
    sent = [value(f"{name} {j}") for name in ("swapped", "beyond") for j in range(parts)]
    sent += [value("swapped other"), value("beyond other")]
    child_column, child_diag = pl.pallas_call(
        child_kernel,
        out_shape=(
            jax.ShapeDtypeStruct(l_child.shape, BF16),
            jax.ShapeDtypeStruct(dinv_child.shape, BF16),
        ),
        in_specs=[smem] * 3 + [vmem] * 4 + [hbm] * (len(sent) + 2),
        out_specs=(hbm,) * 2,
        scratch_shapes=[
            pltpu.VMEM((children, 2, parts, rows, half), BF16),
            pltpu.VMEM((children, tops, half), BF16),
            pltpu.VMEM((children, tops, half), BF16),
            pltpu.VMEM((children, width, half), BF16),
            pltpu.VMEM((children, width, half), BF16),
            pltpu.SemaphoreType.DMA((24,)),
        ],
        compiler_params=pltpu.CompilerParams(vmem_limit_bytes=20 << 20),
    )(
        place, slot, keep_child, full, l_child, value("c other"), dinv_child,
        whole, value("own other"), *sent,
    )
    return parent_diag[None], child_column, child_diag


def solution(mesh):
    blocks = P(("poles", "row"), None, "col")
    placed = (
        P(("poles", "row", "col"), None),
        blocks,
        blocks,
        P(("poles", "row"), None),
        blocks,
        blocks,
        P(("poles", "row"), None),
        P(("poles", "row")),
    )
    return jax.shard_map(
        local, mesh=mesh, in_specs=placed, out_specs=(blocks,) * 3, check_vma=False
    )
```

```python
import functools

import jax
import jax.numpy as jnp
from jax import lax
from jax.experimental import pallas as pl
from jax.experimental.pallas import tpu as pltpu
from jax.sharding import PartitionSpec as P

DIRECT = 4
F32 = jnp.float32
BF16 = jnp.bfloat16
SEQUENCES = (
    (1, (
        "near other",
        "far other",
    )),
    (1, (
        "a 2",
        "c other",
    )),
    (1, (
        "a 2",
        "own other",
    )),
)


def dot(a, b):
    return jnp.dot(a, b, preferred_element_type=F32)


def dot_t(a, b):
    return lax.dot_general(a, b, (((0,), (0,)), ((), ())), preferred_element_type=F32)


class Loads:
    def __init__(self, sem):
        self.sem, self.used = sem, 0

    def start(self, src, dst):
        copy = pltpu.make_async_copy(src, dst, self.sem.at[self.used])
        self.used += 1
        copy.start()
        return copy

    def choose(self, which, srcs, dst):
        sem = self.sem.at[self.used]
        self.used += 1
        for k, src in enumerate(srcs):

            @pl.when(which == k)
            def _(src=src):
                pltpu.make_async_copy(src, dst, sem).start()

        return pltpu.make_async_copy(srcs[0], dst, sem)


def wait(copies):
    for copy in copies:
        copy.wait()


def pack_kernel(keep_ref, factor, inverse, *refs):
    parts, whole, sem = refs[:-2], refs[-2], refs[-1]
    width = inverse.shape[0]
    share = width // len(parts)
    loads = Loads(sem)
    copies = [
        (
            loads.start(factor.at[pl.ds(i * width, width)], part.at[pl.ds(0, width)]),
            loads.start(inverse.at[pl.ds(i * share, share)], part.at[pl.ds(width, share)]),
        )
        for i, part in enumerate(parts)
    ]
    for i, part in enumerate(parts):
        wait(copies[i])

        @pl.when(keep_ref[0, i] == 0)
        def _(part=part):
            part[pl.ds(0, width), :] = jnp.zeros((width, part.shape[1]), part.dtype)

        whole[i] = part[...]


def load_top(loads, place, near, near_o, far, far_o, a, b):
    planes, block = near.shape[:2]
    me, at, pair = place
    copies = []
    for i, ref in enumerate((far, far_o)):
        copies.append(loads.start(ref, b.at[i]))
    for ref, core in ((near, me), (near_o, 1 - me)):
        for k in range(planes):
            plane = lax.rem(at + planes - k, planes)
            row = pl.multiple_of(((plane * 2 + pair) * 2 + core) * block, block)
            copies.append(loads.start(ref.at[k], a.at[pl.ds(row, block)]))
    return copies


def place_top(place, a, b):
    me, at, mine_at = place
    _, planes, block, _ = b.shape
    span = 2 * block
    for pair in range(2):

        @pl.when(mine_at == pair)
        def _():
            for k in range(planes):
                plane = lax.rem(at + planes - k, planes)
                for i, core in enumerate((me, 1 - me)):
                    row = pl.multiple_of(((plane * 2 + 1 - pair) * 2 + core) * block, block)
                    for j in range(planes):
                        col = (2 * j + 1 - pair) * span
                        a[pl.ds(row, block), col : col + span] = b[i, k, :, j * span : (j + 1) * span]
            for i in range(planes):
                for j in range(planes):
                    mine = (2 * i + pair) * span
                    theirs = (2 * j + 1 - pair) * span
                    a[theirs : theirs + span, mine : mine + span] = a[
                        mine : mine + span, theirs : theirs + span
                    ].T


def place_of():
    row = lax.axis_index("row")
    return lax.axis_index("col"), lax.div(row, 2), lax.rem(row, 2)


def sides_of(me, half):
    mine = pl.multiple_of(me * half, half)
    other = pl.multiple_of((1 - me) * half, half)
    return pl.ds(mine, half), pl.ds(other, half)


def parent_kernel(*refs, direct):
    place = place_of()
    if direct:
        a_refs, refs = refs[:4], refs[4:]
    else:
        a_refs, refs = refs[:1], refs[1:]
    own, own_o, dp, pd, a, b, g, sem = refs
    width, half = dp.shape
    parts = own.shape[0]
    loads = Loads(sem)
    if direct:
        wait(load_top(loads, place, *a_refs, a, b))
        place_top(place, a, b)
    else:
        loads.start(a_refs[0], a).wait()
    head = pl.ds(0, width)
    total = dot(a[:, :width], own[0, head, :])
    for j in range(1, parts):
        total += dot(a[:, j * width : (j + 1) * width], own[j, head, :])
    g[...] = total.astype(BF16)
    for r, at in zip((own, own_o), sides_of(place[0], half)):
        y = dp[at, :].astype(F32)
        for j in range(parts):
            y += dot_t(r[j, head, :], g[j * width : (j + 1) * width, :])
        pd[at, :] = y.astype(BF16)


def child_kernel(parent_ref, keep_ref, a, lc, lc_o, dc, own, own_o, *refs):
    parts = own.shape[0]
    swapped, beyond, refs = refs[:parts], refs[parts : 2 * parts], refs[2 * parts :]
    swapped_o, beyond_o, refs = refs[0], refs[1], refs[2:]
    cc_out, cd_out, x, co, v, t, cc, cd, sem = refs
    children, _, half = lc.shape
    width = 2 * half
    tops = a.shape[0]
    head, below, tail = pl.ds(0, width), pl.ds(width, tops), pl.ds(width, half)
    me, row = lax.axis_index("col"), lax.axis_index("row")
    ends = sides_of(me, half)
    holds = (me, 1 - me)
    pair = row + 1 - 2 * lax.rem(row, 2)
    loads = Loads(sem)
    chosen, outs = [], []
    for k in range(children):
        parent = parent_ref[k]
        slot = jnp.where(parent == row, 0, jnp.where(parent == pair, 1, 2))
        chosen.append([])
        for j in range(parts):
            for i, srcs in enumerate(
                (
                    (own.at[j], swapped[j], beyond[j]),
                    (own_o.at[j], swapped_o.at[j], beyond_o.at[j]),
                )
            ):
                chosen[k].append(loads.choose(slot, srcs, x.at[k, i, j]))
    panel_o = loads.start(lc_o, co)
    for k in range(children):
        wait(chosen[k])
        for j in range(parts):
            rows = pl.ds(j * width, width)
            w = lc[k, pl.ds(width + j * width, width), :].astype(F32)
            part = dot(x[k, 0, j, head, :], lc[k, ends[0], :])
            part += dot(x[k, 1, j, head, :], lc[k, ends[1], :])
            v[k, rows, :] = (part - jnp.where(keep_ref[k, j] > 0, w, 0.0)).astype(BF16)
    for k in range(children):
        t[k] = dot(a[...], v[k]).astype(BF16)
    for k in range(children):
        for i in range(2):
            y = dot(x[k, 0, holds[i], tail, :], lc[k, ends[0], :])
            y += dot(x[k, 1, holds[i], tail, :], lc[k, ends[1], :])
            for j in range(parts):
                y += dot_t(x[k, i, j, head, :], t[k, j * width : (j + 1) * width, :])
            cc[k, ends[i], :] = (-y).astype(BF16)
        outs.append(loads.start(cc.at[k], cc_out.at[k, head]))
        for j in range(parts):

            @pl.when(keep_ref[k, j] == 0)
            def _(k=k, j=j):
                t[k, pl.ds(j * width, width), :] = jnp.zeros((width, half), BF16)

        outs.append(loads.start(t.at[k], cc_out.at[k, below]))
    panel_o.wait()
    for k in range(children):
        for i, r in enumerate((lc, co)):
            y = dot_t(r[k, below, :], t[k]) + dot_t(r[k, head, :], cc[k])
            cd[k, ends[i], :] = (dc[k, ends[i], :].astype(F32) - y).astype(BF16)
        outs.append(loads.start(cd.at[k], cd_out.at[k]))
    wait(outs)


def local(ainv_top, l_parent, dinv_parent, keep_parent, l_child, dinv_child, keep_child, parent_of):
    devices = lax.axis_size("row")
    planes = devices // 2
    row = lax.axis_index("row")
    swap = [(i, i ^ 1) for i in range(devices)]
    onward = [(i, i - 2 if i % 2 else i + 2) for i in range(devices)]
    onward = [(i, j) for i, j in onward if 0 <= j < devices]
    cores = [(0, 1), (1, 0)]
    half = l_parent.shape[2]
    width = 2 * half
    tops = l_parent.shape[1]
    parts = tops // width
    rows = width + width // parts
    children = l_child.shape[0]
    direct = planes <= DIRECT
    smem = pl.BlockSpec(memory_space=pltpu.SMEM)
    vmem = pl.BlockSpec(memory_space=pltpu.VMEM)
    hbm = pl.BlockSpec(memory_space=pl.ANY)
    packed = jax.ShapeDtypeStruct((rows, half), BF16)
    *own, whole = pl.pallas_call(
        pack_kernel,
        out_shape=(packed,) * parts + (jax.ShapeDtypeStruct((parts, rows, half), BF16),),
        in_specs=[smem] + [pl.BlockSpec(memory_space=pltpu.HBM)] * 2,
        out_specs=(vmem,) * (parts + 1),
        scratch_shapes=[pltpu.SemaphoreType.DMA((2 * parts,))],
        compiler_params=pltpu.CompilerParams(vmem_limit_bytes=60 << 20),
    )(keep_parent, l_parent[0], dinv_parent[0])
    ainv_top, *own = lax.optimization_barrier((ainv_top, *own))
    got = {"own": whole, "c": l_child, "a": ainv_top}
    got.update((f"own {j}", own[j]) for j in range(parts))

    moves = {}
    for j in range(parts):
        moves[f"swapped {j}"] = (f"own {j}", "row", swap)
        moves[f"beyond {j}"] = (f"swapped {j}", "row", onward)
    for name in ("own", "c", "swapped", "beyond"):
        moves[name + " other"] = (name, "col", cores)
    if direct:
        for k in range(1, planes):
            moves[f"a {k}"] = ("a", "row", [(i, (i + 2 * k) % devices) for i in range(devices)])
        moves["far"] = ("sides", "row", swap)
        moves["near other"] = ("near", "col", cores)
        moves["far other"] = ("far", "col", cores)

    def value(name):
        if name in got:
            return got[name]
        if name in ("swapped", "beyond"):
            got[name] = jnp.stack([value(f"{name} {j}") for j in range(parts)])
        elif name in ("near", "sides"):
            near = jnp.stack([got["a"], *(value(f"a {k}") for k in range(1, planes))])
            sides = near.reshape(planes, near.shape[1], planes, 2, -1)
            sides = jnp.where(row % 2 == 0, sides[:, :, :, 0], sides[:, :, :, 1])
            got["near"] = near
            got["sides"] = sides.reshape(planes, near.shape[1], -1)
        else:
            source, axis, pairs = moves[name]
            got[name] = lax.ppermute(value(source), axis, pairs)
        return got[name]

    for window, sequence in SEQUENCES:
        sequence = [name for name in sequence if name in moves]
        for i, name in enumerate(sequence):
            if name in got:
                continue
            source, axis, pairs = moves[name]
            sent = value(source)
            if i >= window:
                sent = lax.optimization_barrier((sent, value(sequence[i - window])))[0]
            got[name] = lax.ppermute(sent, axis, pairs)
    if direct:
        top = [value(name) for name in ("near", "near other", "far", "far other")]
    else:
        top = [lax.all_gather(ainv_top, ("row", "col"), axis=0, tiled=True)]
    parent_diag, full = pl.pallas_call(
        functools.partial(parent_kernel, direct=direct),
        out_shape=(
            jax.ShapeDtypeStruct((width, half), BF16),
            jax.ShapeDtypeStruct((tops, tops), BF16),
        ),
        in_specs=[hbm] * len(top) + [vmem] * 3,
        out_specs=(vmem,) * 2,
        scratch_shapes=[
            pltpu.VMEM((2, *top[-1].shape) if direct else (16, half), BF16),
            pltpu.VMEM((tops, half), BF16),
            pltpu.SemaphoreType.DMA((4 * devices if direct else 1,)),
        ],
        compiler_params=pltpu.CompilerParams(vmem_limit_bytes=12 << 20),
        cost_estimate=pl.CostEstimate(
            flops=2 * tops * half * (tops + width), bytes_accessed=8 << 20, transcendentals=0
        ),
    )(*top, whole, value("own other"), dinv_parent[0])
    sent = [value(f"{name} {j}") for name in ("swapped", "beyond") for j in range(parts)]
    sent += [value("swapped other"), value("beyond other")]
    child_column, child_diag = pl.pallas_call(
        child_kernel,
        out_shape=(
            jax.ShapeDtypeStruct(l_child.shape, BF16),
            jax.ShapeDtypeStruct(dinv_child.shape, BF16),
        ),
        in_specs=[smem] * 2 + [vmem] * 2 + [hbm, vmem] + [hbm] * (len(sent) + 2),
        out_specs=(hbm,) * 2,
        scratch_shapes=[
            pltpu.VMEM((children, 2, parts, rows, half), BF16),
            pltpu.VMEM(l_child.shape, BF16),
            pltpu.VMEM((children, tops, half), BF16),
            pltpu.VMEM((children, tops, half), BF16),
            pltpu.VMEM((children, width, half), BF16),
            pltpu.VMEM((children, width, half), BF16),
            pltpu.SemaphoreType.DMA((24,)),
        ],
        compiler_params=pltpu.CompilerParams(vmem_limit_bytes=20 << 20),
    )(
        parent_of, keep_child, full, l_child, value("c other"), dinv_child,
        whole, value("own other"), *sent,
    )
    return parent_diag[None], child_column, child_diag


def solution(mesh):
    blocks = P(("poles", "row"), None, "col")
    placed = (
        P(("poles", "row", "col"), None),
        blocks,
        blocks,
        P(("poles", "row"), None),
        blocks,
        blocks,
        P(("poles", "row"), None),
        P(("poles", "row")),
    )
    return jax.shard_map(
        local, mesh=mesh, in_specs=placed, out_specs=(blocks,) * 3, check_vma=False
    )
```

```python
import functools

import jax
import jax.numpy as jnp
from jax import lax
from jax.experimental import pallas as pl
from jax.experimental.pallas import tpu as pltpu
from jax.sharding import PartitionSpec as P

DIRECT = 4
F32 = jnp.float32
BF16 = jnp.bfloat16
SEQUENCES = (
    (1, (
        "near other",
        "far other",
    )),
    (1, (
        "a 2",
        "c other",
    )),
    (1, (
        "a 2",
        "own other",
    )),
)


def dot(a, b):
    return jnp.dot(a, b, preferred_element_type=F32)


def dot_t(a, b):
    return lax.dot_general(a, b, (((0,), (0,)), ((), ())), preferred_element_type=F32)


class Loads:
    def __init__(self, sem):
        self.sem, self.used = sem, 0

    def start(self, src, dst):
        copy = pltpu.make_async_copy(src, dst, self.sem.at[self.used])
        self.used += 1
        copy.start()
        return copy


def wait(copies):
    for copy in copies:
        copy.wait()


def pack_kernel(keep_ref, factor, inverse, *refs):
    parts, (whole, x, sem) = refs[:-3], refs[-3:]
    width = inverse.shape[0]
    share = width // len(parts)
    loads = Loads(sem)
    copies = [
        (
            loads.start(factor.at[pl.ds(i * width, width)], x.at[i, pl.ds(0, width)]),
            loads.start(inverse.at[pl.ds(i * share, share)], x.at[i, pl.ds(width, share)]),
        )
        for i in range(len(parts))
    ]
    outs = []
    for i, part in enumerate(parts):
        wait(copies[i])

        @pl.when(keep_ref[0, i] == 0)
        def _(i=i):
            x[i, pl.ds(0, width), :] = jnp.zeros((width, x.shape[2]), x.dtype)

        outs.append(loads.start(x.at[i], part))
    outs.append(loads.start(x, whole))
    wait(outs)


def load_top(loads, place, near, near_o, far, far_o, a, b):
    planes, block = near.shape[:2]
    me, at, pair = place
    copies = []
    for i, ref in enumerate((far, far_o)):
        copies.append(loads.start(ref, b.at[i]))
    for ref, core in ((near, me), (near_o, 1 - me)):
        for k in range(planes):
            plane = lax.rem(at + planes - k, planes)
            row = pl.multiple_of(((plane * 2 + pair) * 2 + core) * block, block)
            copies.append(loads.start(ref.at[k], a.at[pl.ds(row, block)]))
    return copies


def place_top(place, a, b):
    me, at, mine_at = place
    _, planes, block, _ = b.shape
    span = 2 * block
    for pair in range(2):

        @pl.when(mine_at == pair)
        def _():
            for k in range(planes):
                plane = lax.rem(at + planes - k, planes)
                for i, core in enumerate((me, 1 - me)):
                    row = pl.multiple_of(((plane * 2 + 1 - pair) * 2 + core) * block, block)
                    for j in range(planes):
                        col = (2 * j + 1 - pair) * span
                        a[pl.ds(row, block), col : col + span] = b[i, k, :, j * span : (j + 1) * span]
            for i in range(planes):
                for j in range(planes):
                    mine = (2 * i + pair) * span
                    theirs = (2 * j + 1 - pair) * span
                    a[theirs : theirs + span, mine : mine + span] = a[
                        mine : mine + span, theirs : theirs + span
                    ].T


def place_of():
    row = lax.axis_index("row")
    return lax.axis_index("col"), lax.div(row, 2), lax.rem(row, 2)


def sides_of(me, half):
    mine = pl.multiple_of(me * half, half)
    other = pl.multiple_of((1 - me) * half, half)
    return pl.ds(mine, half), pl.ds(other, half)


def parent_kernel(*refs, direct):
    place = place_of()
    if direct:
        a_refs, refs = refs[:4], refs[4:]
    else:
        a_refs, refs = refs[:1], refs[1:]
    own, own_o, dp, pd, a, b, g, sem = refs
    width, half = dp.shape
    parts = own.shape[0]
    loads = Loads(sem)
    if direct:
        wait(load_top(loads, place, *a_refs, a, b))
        place_top(place, a, b)
    else:
        loads.start(a_refs[0], a).wait()
    head = pl.ds(0, width)
    total = dot(a[:, :width], own[0, head, :])
    for j in range(1, parts):
        total += dot(a[:, j * width : (j + 1) * width], own[j, head, :])
    g[...] = total.astype(BF16)
    for r, at in zip((own, own_o), sides_of(place[0], half)):
        y = dp[at, :].astype(F32)
        for j in range(parts):
            y += dot_t(r[j, head, :], g[j * width : (j + 1) * width, :])
        pd[at, :] = y.astype(BF16)


def child_kernel(parent_ref, keep_ref, a, lc, lc_o, dc, own, own_o, *refs):
    parts = own.shape[0]
    swapped, beyond, refs = refs[:parts], refs[parts : 2 * parts], refs[2 * parts :]
    swapped_o, beyond_o, refs = refs[0], refs[1], refs[2:]
    cc_out, cd_out, x, co, v, t, cc, cd, sem = refs
    children, _, half = lc.shape
    width = 2 * half
    tops = a.shape[0]
    head, below, tail = pl.ds(0, width), pl.ds(width, tops), pl.ds(width, half)
    me, row = lax.axis_index("col"), lax.axis_index("row")
    ends = sides_of(me, half)
    holds = (me, 1 - me)
    pair = row + 1 - 2 * lax.rem(row, 2)
    loads = Loads(sem)
    chosen, outs = [], []
    for k in range(children):
        parent = parent_ref[k]
        sources = (
            (parent == row, [own.at[j] for j in range(parts)], own_o),
            (parent == pair, swapped, swapped_o),
            (jnp.logical_and(parent != row, parent != pair), beyond, beyond_o),
        )
        sems = [sem.at[loads.used + j] for j in range(parts + 1)]
        loads.used += parts + 1
        for flag, mine, other in sources:

            @pl.when(flag)
            def _(k=k, mine=mine, other=other, sems=sems):
                for j in range(parts):
                    pltpu.make_async_copy(mine[j], x.at[k, 0, j], sems[j]).start()
                pltpu.make_async_copy(other, x.at[k, 1], sems[parts]).start()

        chosen.append(
            [pltpu.make_async_copy(own.at[j], x.at[k, 0, j], sems[j]) for j in range(parts)]
            + [pltpu.make_async_copy(own_o, x.at[k, 1], sems[parts])]
        )
    panel_o = loads.start(lc_o, co)
    for k in range(children):
        wait(chosen[k])
        for j in range(parts):
            rows = pl.ds(j * width, width)
            w = lc[k, pl.ds(width + j * width, width), :].astype(F32)
            part = dot(x[k, 0, j, head, :], lc[k, ends[0], :])
            part += dot(x[k, 1, j, head, :], lc[k, ends[1], :])
            v[k, rows, :] = (part - jnp.where(keep_ref[k, j] > 0, w, 0.0)).astype(BF16)
    for k in range(children):
        t[k] = dot(a[...], v[k]).astype(BF16)
    for k in range(children):
        for i in range(2):
            y = dot(x[k, 0, holds[i], tail, :], lc[k, ends[0], :])
            y += dot(x[k, 1, holds[i], tail, :], lc[k, ends[1], :])
            for j in range(parts):
                y += dot_t(x[k, i, j, head, :], t[k, j * width : (j + 1) * width, :])
            cc[k, ends[i], :] = (-y).astype(BF16)
        outs.append(loads.start(cc.at[k], cc_out.at[k, head]))
        for j in range(parts):

            @pl.when(keep_ref[k, j] == 0)
            def _(k=k, j=j):
                t[k, pl.ds(j * width, width), :] = jnp.zeros((width, half), BF16)

        outs.append(loads.start(t.at[k], cc_out.at[k, below]))
    panel_o.wait()
    for k in range(children):
        for i, r in enumerate((lc, co)):
            y = dot_t(r[k, below, :], t[k]) + dot_t(r[k, head, :], cc[k])
            cd[k, ends[i], :] = (dc[k, ends[i], :].astype(F32) - y).astype(BF16)
        outs.append(loads.start(cd.at[k], cd_out.at[k]))
    wait(outs)


def local(ainv_top, l_parent, dinv_parent, keep_parent, l_child, dinv_child, keep_child, parent_of):
    devices = lax.axis_size("row")
    planes = devices // 2
    row = lax.axis_index("row")
    swap = [(i, i ^ 1) for i in range(devices)]
    onward = [(i, i - 2 if i % 2 else i + 2) for i in range(devices)]
    onward = [(i, j) for i, j in onward if 0 <= j < devices]
    cores = [(0, 1), (1, 0)]
    half = l_parent.shape[2]
    width = 2 * half
    tops = l_parent.shape[1]
    parts = tops // width
    rows = width + width // parts
    children = l_child.shape[0]
    direct = planes <= DIRECT
    smem = pl.BlockSpec(memory_space=pltpu.SMEM)
    vmem = pl.BlockSpec(memory_space=pltpu.VMEM)
    hbm = pl.BlockSpec(memory_space=pl.ANY)
    packed = jax.ShapeDtypeStruct((rows, half), BF16)
    *own, whole = pl.pallas_call(
        pack_kernel,
        out_shape=(packed,) * parts + (jax.ShapeDtypeStruct((parts, rows, half), BF16),),
        in_specs=[smem] + [pl.BlockSpec(memory_space=pltpu.HBM)] * 2,
        out_specs=(hbm,) * (parts + 1),
        scratch_shapes=[
            pltpu.VMEM((parts, rows, half), BF16),
            pltpu.SemaphoreType.DMA((3 * parts + 1,)),
        ],
        compiler_params=pltpu.CompilerParams(vmem_limit_bytes=60 << 20),
    )(keep_parent, l_parent[0], dinv_parent[0])
    ainv_top, *own = lax.optimization_barrier((ainv_top, *own))
    got = {"own": whole, "c": l_child, "a": ainv_top}
    got.update((f"own {j}", own[j]) for j in range(parts))

    moves = {}
    for j in range(parts):
        moves[f"swapped {j}"] = (f"own {j}", "row", swap)
        moves[f"beyond {j}"] = (f"swapped {j}", "row", onward)
    for name in ("own", "c", "swapped", "beyond"):
        moves[name + " other"] = (name, "col", cores)
    if direct:
        for k in range(1, planes):
            moves[f"a {k}"] = ("a", "row", [(i, (i + 2 * k) % devices) for i in range(devices)])
        moves["far"] = ("sides", "row", swap)
        moves["near other"] = ("near", "col", cores)
        moves["far other"] = ("far", "col", cores)

    def value(name):
        if name in got:
            return got[name]
        if name in ("swapped", "beyond"):
            got[name] = jnp.stack([value(f"{name} {j}") for j in range(parts)])
        elif name in ("near", "sides"):
            near = jnp.stack([got["a"], *(value(f"a {k}") for k in range(1, planes))])
            sides = near.reshape(planes, near.shape[1], planes, 2, -1)
            sides = jnp.where(row % 2 == 0, sides[:, :, :, 0], sides[:, :, :, 1])
            got["near"] = near
            got["sides"] = sides.reshape(planes, near.shape[1], -1)
        else:
            source, axis, pairs = moves[name]
            got[name] = lax.ppermute(value(source), axis, pairs)
        return got[name]

    for window, sequence in SEQUENCES:
        sequence = [name for name in sequence if name in moves]
        for i, name in enumerate(sequence):
            if name in got:
                continue
            source, axis, pairs = moves[name]
            sent = value(source)
            if i >= window:
                sent = lax.optimization_barrier((sent, value(sequence[i - window])))[0]
            got[name] = lax.ppermute(sent, axis, pairs)
    if direct:
        top = [value(name) for name in ("near", "near other", "far", "far other")]
    else:
        top = [lax.all_gather(ainv_top, ("row", "col"), axis=0, tiled=True)]
    parent_diag, full = pl.pallas_call(
        functools.partial(parent_kernel, direct=direct),
        out_shape=(
            jax.ShapeDtypeStruct((width, half), BF16),
            jax.ShapeDtypeStruct((tops, tops), BF16),
        ),
        in_specs=[hbm] * len(top) + [vmem] * 3,
        out_specs=(vmem,) * 2,
        scratch_shapes=[
            pltpu.VMEM((2, *top[-1].shape) if direct else (16, half), BF16),
            pltpu.VMEM((tops, half), BF16),
            pltpu.SemaphoreType.DMA((4 * devices if direct else 1,)),
        ],
        compiler_params=pltpu.CompilerParams(vmem_limit_bytes=12 << 20),
        cost_estimate=pl.CostEstimate(
            flops=2 * tops * half * (tops + width), bytes_accessed=8 << 20, transcendentals=0
        ),
    )(*top, whole, value("own other"), dinv_parent[0])
    sent = [value(f"{name} {j}") for name in ("swapped", "beyond") for j in range(parts)]
    sent += [value("swapped other"), value("beyond other")]
    child_column, child_diag = pl.pallas_call(
        child_kernel,
        out_shape=(
            jax.ShapeDtypeStruct(l_child.shape, BF16),
            jax.ShapeDtypeStruct(dinv_child.shape, BF16),
        ),
        in_specs=[smem] * 2 + [vmem] * 2 + [hbm, vmem] + [hbm] * (len(sent) + 2),
        out_specs=(hbm,) * 2,
        scratch_shapes=[
            pltpu.VMEM((children, 2, parts, rows, half), BF16),
            pltpu.VMEM(l_child.shape, BF16),
            pltpu.VMEM((children, tops, half), BF16),
            pltpu.VMEM((children, tops, half), BF16),
            pltpu.VMEM((children, width, half), BF16),
            pltpu.VMEM((children, width, half), BF16),
            pltpu.SemaphoreType.DMA((24,)),
        ],
        compiler_params=pltpu.CompilerParams(vmem_limit_bytes=20 << 20),
    )(
        parent_of, keep_child, full, l_child, value("c other"), dinv_child,
        whole, value("own other"), *sent,
    )
    return parent_diag[None], child_column, child_diag


def solution(mesh):
    blocks = P(("poles", "row"), None, "col")
    placed = (
        P(("poles", "row", "col"), None),
        blocks,
        blocks,
        P(("poles", "row"), None),
        blocks,
        blocks,
        P(("poles", "row"), None),
        P(("poles", "row")),
    )
    return jax.shard_map(
        local, mesh=mesh, in_specs=placed, out_specs=(blocks,) * 3, check_vma=False
    )
```

```python
import functools

import jax
import jax.numpy as jnp
from jax import lax
from jax.experimental import pallas as pl
from jax.experimental.pallas import tpu as pltpu
from jax.sharding import PartitionSpec as P

DIRECT = 4
F32 = jnp.float32
BF16 = jnp.bfloat16
SEQUENCES = (
    (1, (
        "near other",
        "far other",
    )),
    (1, (
        "a 2",
        "far other",
    )),
    (1, (
        "beyond 0",
        "own other",
    )),
)


def dot(a, b):
    return jnp.dot(a, b, preferred_element_type=F32)


def dot_t(a, b):
    return lax.dot_general(a, b, (((0,), (0,)), ((), ())), preferred_element_type=F32)


class Loads:
    def __init__(self, sem):
        self.sem, self.used = sem, 0

    def start(self, src, dst):
        copy = pltpu.make_async_copy(src, dst, self.sem.at[self.used])
        self.used += 1
        copy.start()
        return copy


def wait(copies):
    for copy in copies:
        copy.wait()


def pack_kernel(keep_ref, factor, inverse, *refs):
    parts, (whole, x, sem) = refs[:-3], refs[-3:]
    width = inverse.shape[0]
    share = width // len(parts)
    loads = Loads(sem)
    copies = [
        (
            loads.start(factor.at[pl.ds(i * width, width)], x.at[i, pl.ds(0, width)]),
            loads.start(inverse.at[pl.ds(i * share, share)], x.at[i, pl.ds(width, share)]),
        )
        for i in range(len(parts))
    ]
    outs = []
    for i, part in enumerate(parts):
        wait(copies[i])

        @pl.when(keep_ref[0, i] == 0)
        def _(i=i):
            x[i, pl.ds(0, width), :] = jnp.zeros((width, x.shape[2]), x.dtype)

        outs.append(loads.start(x.at[i], part))
    outs.append(loads.start(x, whole))
    wait(outs)


def load_top(loads, place, near, near_o, far, far_o, a, b):
    planes, block = near.shape[:2]
    me, at, pair = place
    copies = []
    for i, ref in enumerate((far, far_o)):
        copies.append(loads.start(ref, b.at[i]))
    for ref, core in ((near, me), (near_o, 1 - me)):
        for k in range(planes):
            plane = lax.rem(at + planes - k, planes)
            row = pl.multiple_of(((plane * 2 + pair) * 2 + core) * block, block)
            copies.append(loads.start(ref.at[k], a.at[pl.ds(row, block)]))
    return copies


def place_top(place, a, b):
    me, at, mine_at = place
    _, planes, block, _ = b.shape
    span = 2 * block
    for pair in range(2):

        @pl.when(mine_at == pair)
        def _():
            for k in range(planes):
                plane = lax.rem(at + planes - k, planes)
                for i, core in enumerate((me, 1 - me)):
                    row = pl.multiple_of(((plane * 2 + 1 - pair) * 2 + core) * block, block)
                    for j in range(planes):
                        col = (2 * j + 1 - pair) * span
                        a[pl.ds(row, block), col : col + span] = b[i, k, :, j * span : (j + 1) * span]
            for i in range(planes):
                for j in range(planes):
                    mine = (2 * i + pair) * span
                    theirs = (2 * j + 1 - pair) * span
                    a[theirs : theirs + span, mine : mine + span] = a[
                        mine : mine + span, theirs : theirs + span
                    ].T


def place_of():
    row = lax.axis_index("row")
    return lax.axis_index("col"), lax.div(row, 2), lax.rem(row, 2)


def sides_of(me, half):
    mine = pl.multiple_of(me * half, half)
    other = pl.multiple_of((1 - me) * half, half)
    return pl.ds(mine, half), pl.ds(other, half)


def parent_kernel(*refs, direct):
    place = place_of()
    if direct:
        a_refs, refs = refs[:4], refs[4:]
    else:
        a_refs, refs = refs[:1], refs[1:]
    own, own_o, dp, pd, a, b, g, sem = refs
    width, half = dp.shape
    parts = own.shape[0]
    loads = Loads(sem)
    if direct:
        wait(load_top(loads, place, *a_refs, a, b))
        place_top(place, a, b)
    else:
        loads.start(a_refs[0], a).wait()
    head = pl.ds(0, width)
    total = dot(a[:, :width], own[0, head, :])
    for j in range(1, parts):
        total += dot(a[:, j * width : (j + 1) * width], own[j, head, :])
    g[...] = total.astype(BF16)
    for r, at in zip((own, own_o), sides_of(place[0], half)):
        y = dp[at, :].astype(F32)
        for j in range(parts):
            y += dot_t(r[j, head, :], g[j * width : (j + 1) * width, :])
        pd[at, :] = y.astype(BF16)


def child_kernel(parent_ref, keep_ref, a, lc, lc_o, dc, own, own_o, *refs):
    parts = own.shape[0]
    swapped, beyond, refs = refs[:parts], refs[parts : 2 * parts], refs[2 * parts :]
    swapped_o, beyond_o, refs = refs[0], refs[1], refs[2:]
    cc_out, cd_out, x, co, v, t, cc, cd, sem = refs
    children, _, half = lc.shape
    width = 2 * half
    tops = a.shape[0]
    head, below, tail = pl.ds(0, width), pl.ds(width, tops), pl.ds(width, half)
    me, row = lax.axis_index("col"), lax.axis_index("row")
    ends = sides_of(me, half)
    holds = (me, 1 - me)
    pair = row + 1 - 2 * lax.rem(row, 2)
    loads = Loads(sem)
    chosen, outs = [], []
    for k in range(children):
        parent = parent_ref[k]
        sources = (
            (parent == row, [own.at[j] for j in range(parts)], own_o),
            (parent == pair, swapped, swapped_o),
            (jnp.logical_and(parent != row, parent != pair), beyond, beyond_o),
        )
        sems = [sem.at[loads.used + j] for j in range(parts + 1)]
        loads.used += parts + 1
        for flag, mine, other in sources:

            @pl.when(flag)
            def _(k=k, mine=mine, other=other, sems=sems):
                for j in range(parts):
                    pltpu.make_async_copy(mine[j], x.at[k, 0, j], sems[j]).start()
                pltpu.make_async_copy(other, x.at[k, 1], sems[parts]).start()

        chosen.append(
            [pltpu.make_async_copy(own.at[j], x.at[k, 0, j], sems[j]) for j in range(parts)]
            + [pltpu.make_async_copy(own_o, x.at[k, 1], sems[parts])]
        )
    panel_o = loads.start(lc_o, co)
    for k in range(children):
        wait(chosen[k])
        for j in range(parts):
            rows = pl.ds(j * width, width)
            w = lc[k, pl.ds(width + j * width, width), :].astype(F32)
            part = dot(x[k, 0, j, head, :], lc[k, ends[0], :])
            part += dot(x[k, 1, j, head, :], lc[k, ends[1], :])
            v[k, rows, :] = (part - jnp.where(keep_ref[k, j] > 0, w, 0.0)).astype(BF16)
    for k in range(children):
        t[k] = dot(a[...], v[k]).astype(BF16)
    for k in range(children):
        for i in range(2):
            y = dot(x[k, 0, holds[i], tail, :], lc[k, ends[0], :])
            y += dot(x[k, 1, holds[i], tail, :], lc[k, ends[1], :])
            for j in range(parts):
                y += dot_t(x[k, i, j, head, :], t[k, j * width : (j + 1) * width, :])
            cc[k, ends[i], :] = (-y).astype(BF16)
        outs.append(loads.start(cc.at[k], cc_out.at[k, head]))
        for j in range(parts):

            @pl.when(keep_ref[k, j] == 0)
            def _(k=k, j=j):
                t[k, pl.ds(j * width, width), :] = jnp.zeros((width, half), BF16)

        outs.append(loads.start(t.at[k], cc_out.at[k, below]))
    panel_o.wait()
    for k in range(children):
        for i, r in enumerate((lc, co)):
            y = dot_t(r[k, below, :], t[k]) + dot_t(r[k, head, :], cc[k])
            cd[k, ends[i], :] = (dc[k, ends[i], :].astype(F32) - y).astype(BF16)
        outs.append(loads.start(cd.at[k], cd_out.at[k]))
    wait(outs)


def local(ainv_top, l_parent, dinv_parent, keep_parent, l_child, dinv_child, keep_child, parent_of):
    devices = lax.axis_size("row")
    planes = devices // 2
    row = lax.axis_index("row")
    swap = [(i, i ^ 1) for i in range(devices)]
    onward = [(i, i - 2 if i % 2 else i + 2) for i in range(devices)]
    onward = [(i, j) for i, j in onward if 0 <= j < devices]
    cores = [(0, 1), (1, 0)]
    half = l_parent.shape[2]
    width = 2 * half
    tops = l_parent.shape[1]
    parts = tops // width
    rows = width + width // parts
    children = l_child.shape[0]
    direct = planes <= DIRECT
    smem = pl.BlockSpec(memory_space=pltpu.SMEM)
    vmem = pl.BlockSpec(memory_space=pltpu.VMEM)
    hbm = pl.BlockSpec(memory_space=pl.ANY)
    packed = jax.ShapeDtypeStruct((rows, half), BF16)
    *own, whole = pl.pallas_call(
        pack_kernel,
        out_shape=(packed,) * parts + (jax.ShapeDtypeStruct((parts, rows, half), BF16),),
        in_specs=[smem] + [pl.BlockSpec(memory_space=pltpu.HBM)] * 2,
        out_specs=(hbm,) * (parts + 1),
        scratch_shapes=[
            pltpu.VMEM((parts, rows, half), BF16),
            pltpu.SemaphoreType.DMA((3 * parts + 1,)),
        ],
        compiler_params=pltpu.CompilerParams(vmem_limit_bytes=60 << 20),
    )(keep_parent, l_parent[0], dinv_parent[0])
    ainv_top, *own = lax.optimization_barrier((ainv_top, *own))
    got = {"own": whole, "c": l_child, "a": ainv_top}
    got.update((f"own {j}", own[j]) for j in range(parts))

    moves = {}
    for j in range(parts):
        moves[f"swapped {j}"] = (f"own {j}", "row", swap)
        moves[f"beyond {j}"] = (f"swapped {j}", "row", onward)
    for name in ("own", "c", "swapped", "beyond"):
        moves[name + " other"] = (name, "col", cores)
    if direct:
        for k in range(1, planes):
            moves[f"a {k}"] = ("a", "row", [(i, (i + 2 * k) % devices) for i in range(devices)])
        moves["far"] = ("sides", "row", swap)
        moves["near other"] = ("near", "col", cores)
        moves["far other"] = ("far", "col", cores)

    def value(name):
        if name in got:
            return got[name]
        if name in ("swapped", "beyond"):
            got[name] = jnp.stack([value(f"{name} {j}") for j in range(parts)])
        elif name in ("near", "sides"):
            near = jnp.stack([got["a"], *(value(f"a {k}") for k in range(1, planes))])
            sides = near.reshape(planes, near.shape[1], planes, 2, -1)
            sides = jnp.where(row % 2 == 0, sides[:, :, :, 0], sides[:, :, :, 1])
            got["near"] = near
            got["sides"] = sides.reshape(planes, near.shape[1], -1)
        else:
            source, axis, pairs = moves[name]
            got[name] = lax.ppermute(value(source), axis, pairs)
        return got[name]

    for window, sequence in SEQUENCES:
        sequence = [name for name in sequence if name in moves]
        for i, name in enumerate(sequence):
            if name in got:
                continue
            source, axis, pairs = moves[name]
            sent = value(source)
            if i >= window:
                sent = lax.optimization_barrier((sent, value(sequence[i - window])))[0]
            got[name] = lax.ppermute(sent, axis, pairs)
    if direct:
        top = [value(name) for name in ("near", "near other", "far", "far other")]
    else:
        top = [lax.all_gather(ainv_top, ("row", "col"), axis=0, tiled=True)]
    parent_diag, full = pl.pallas_call(
        functools.partial(parent_kernel, direct=direct),
        out_shape=(
            jax.ShapeDtypeStruct((width, half), BF16),
            jax.ShapeDtypeStruct((tops, tops), BF16),
        ),
        in_specs=[hbm] * len(top) + [vmem] * 3,
        out_specs=(vmem,) * 2,
        scratch_shapes=[
            pltpu.VMEM((2, *top[-1].shape) if direct else (16, half), BF16),
            pltpu.VMEM((tops, half), BF16),
            pltpu.SemaphoreType.DMA((4 * devices if direct else 1,)),
        ],
        compiler_params=pltpu.CompilerParams(vmem_limit_bytes=12 << 20),
        cost_estimate=pl.CostEstimate(
            flops=2 * tops * half * (tops + width), bytes_accessed=8 << 20, transcendentals=0
        ),
    )(*top, whole, value("own other"), dinv_parent[0])
    sent = [value(f"{name} {j}") for name in ("swapped", "beyond") for j in range(parts)]
    sent += [value("swapped other"), value("beyond other")]
    child_column, child_diag = pl.pallas_call(
        child_kernel,
        out_shape=(
            jax.ShapeDtypeStruct(l_child.shape, BF16),
            jax.ShapeDtypeStruct(dinv_child.shape, BF16),
        ),
        in_specs=[smem] * 2 + [vmem] * 2 + [hbm, vmem] + [hbm] * (len(sent) + 2),
        out_specs=(hbm,) * 2,
        scratch_shapes=[
            pltpu.VMEM((children, 2, parts, rows, half), BF16),
            pltpu.VMEM(l_child.shape, BF16),
            pltpu.VMEM((children, tops, half), BF16),
            pltpu.VMEM((children, tops, half), BF16),
            pltpu.VMEM((children, width, half), BF16),
            pltpu.VMEM((children, width, half), BF16),
            pltpu.SemaphoreType.DMA((24,)),
        ],
        compiler_params=pltpu.CompilerParams(vmem_limit_bytes=20 << 20),
    )(
        parent_of, keep_child, full, l_child, value("c other"), dinv_child,
        whole, value("own other"), *sent,
    )
    return parent_diag[None], child_column, child_diag


def solution(mesh):
    blocks = P(("poles", "row"), None, "col")
    placed = (
        P(("poles", "row", "col"), None),
        blocks,
        blocks,
        P(("poles", "row"), None),
        blocks,
        blocks,
        P(("poles", "row"), None),
        P(("poles", "row")),
    )
    return jax.shard_map(
        local, mesh=mesh, in_specs=placed, out_specs=(blocks,) * 3, check_vma=False
    )
```

```python
import functools

import jax
import jax.numpy as jnp
from jax import lax
from jax.experimental import pallas as pl
from jax.experimental.pallas import tpu as pltpu
from jax.sharding import PartitionSpec as P

DIRECT = 4
F32 = jnp.float32
BF16 = jnp.bfloat16
SEQUENCES = (
    (1, (
        "near other",
        "far other",
    )),
    (1, (
        "a 2",
        "far other",
    )),
    (1, (
        "beyond 0",
        "own other",
    )),
)


def dot(a, b):
    return jnp.dot(a, b, preferred_element_type=F32)


def dot_t(a, b):
    return lax.dot_general(a, b, (((0,), (0,)), ((), ())), preferred_element_type=F32)


class Loads:
    def __init__(self, sem):
        self.sem, self.used = sem, 0

    def start(self, src, dst):
        copy = pltpu.make_async_copy(src, dst, self.sem.at[self.used])
        self.used += 1
        copy.start()
        return copy


def wait(copies):
    for copy in copies:
        copy.wait()


def pack_kernel(keep_ref, factor, inverse, *refs):
    parts, (whole, x, sem) = refs[:-3], refs[-3:]
    width = inverse.shape[0]
    share = width // len(parts)
    loads = Loads(sem)
    copies = [
        (
            loads.start(factor.at[pl.ds(i * width, width)], x.at[i, pl.ds(0, width)]),
            loads.start(inverse.at[pl.ds(i * share, share)], x.at[i, pl.ds(width, share)]),
        )
        for i in range(len(parts))
    ]
    outs = []
    for i, part in enumerate(parts):
        wait(copies[i])

        @pl.when(keep_ref[0, i] == 0)
        def _(i=i):
            x[i, pl.ds(0, width), :] = jnp.zeros((width, x.shape[2]), x.dtype)

        outs.append(loads.start(x.at[i], part))
    outs.append(loads.start(x, whole))
    wait(outs)


def load_top(loads, place, near, near_o, far, far_o, a, b):
    planes, block = near.shape[:2]
    me, at, pair = place
    copies = []
    for ref, core in ((near, me), (near_o, 1 - me)):
        for k in range(planes):
            plane = lax.rem(at + planes - k, planes)
            row = pl.multiple_of(((plane * 2 + pair) * 2 + core) * block, block)
            copies.append(loads.start(ref.at[k], a.at[pl.ds(row, block)]))
    return copies, [loads.start(ref, b.at[i]) for i, ref in enumerate((far, far_o))]


def place_top(place, first, second, a, b):
    me, at, mine_at = place
    _, planes, block, _ = b.shape
    span = 2 * block
    wait(first)
    for pair in range(2):

        @pl.when(mine_at == pair)
        def _():
            for i in range(planes):
                for j in range(planes):
                    mine = (2 * i + pair) * span
                    theirs = (2 * j + 1 - pair) * span
                    a[theirs : theirs + span, mine : mine + span] = a[
                        mine : mine + span, theirs : theirs + span
                    ].T

    wait(second)
    for pair in range(2):

        @pl.when(mine_at == pair)
        def _():
            for k in range(planes):
                plane = lax.rem(at + planes - k, planes)
                for i, core in enumerate((me, 1 - me)):
                    row = pl.multiple_of(((plane * 2 + 1 - pair) * 2 + core) * block, block)
                    for j in range(planes):
                        col = (2 * j + 1 - pair) * span
                        a[pl.ds(row, block), col : col + span] = b[i, k, :, j * span : (j + 1) * span]


def place_of():
    row = lax.axis_index("row")
    return lax.axis_index("col"), lax.div(row, 2), lax.rem(row, 2)


def sides_of(me, half):
    mine = pl.multiple_of(me * half, half)
    other = pl.multiple_of((1 - me) * half, half)
    return pl.ds(mine, half), pl.ds(other, half)


def parent_kernel(*refs, direct):
    place = place_of()
    if direct:
        a_refs, refs = refs[:4], refs[4:]
    else:
        a_refs, refs = refs[:1], refs[1:]
    own, own_o, dp, pd, a, b, g, sem = refs
    width, half = dp.shape
    parts = own.shape[0]
    loads = Loads(sem)
    if direct:
        place_top(place, *load_top(loads, place, *a_refs, a, b), a, b)
    else:
        loads.start(a_refs[0], a).wait()
    head = pl.ds(0, width)
    total = dot(a[:, :width], own[0, head, :])
    for j in range(1, parts):
        total += dot(a[:, j * width : (j + 1) * width], own[j, head, :])
    g[...] = total.astype(BF16)
    for r, at in zip((own, own_o), sides_of(place[0], half)):
        y = dp[at, :].astype(F32)
        for j in range(parts):
            y += dot_t(r[j, head, :], g[j * width : (j + 1) * width, :])
        pd[at, :] = y.astype(BF16)


def child_kernel(parent_ref, keep_ref, a, lc, lc_o, dc, own, own_o, *refs):
    parts = own.shape[0]
    swapped, beyond, refs = refs[:parts], refs[parts : 2 * parts], refs[2 * parts :]
    swapped_o, beyond_o, refs = refs[0], refs[1], refs[2:]
    cc_out, cd_out, x, co, v, t, cc, cd, sem = refs
    children, _, half = lc.shape
    width = 2 * half
    tops = a.shape[0]
    head, below, tail = pl.ds(0, width), pl.ds(width, tops), pl.ds(width, half)
    me, row = lax.axis_index("col"), lax.axis_index("row")
    ends = sides_of(me, half)
    holds = (me, 1 - me)
    pair = row + 1 - 2 * lax.rem(row, 2)
    loads = Loads(sem)
    chosen, outs = [], []
    for k in range(children):
        parent = parent_ref[k]
        sources = (
            (parent == row, [own.at[j] for j in range(parts)], own_o),
            (parent == pair, swapped, swapped_o),
            (jnp.logical_and(parent != row, parent != pair), beyond, beyond_o),
        )
        sems = [sem.at[loads.used + j] for j in range(parts + 1)]
        loads.used += parts + 1
        for flag, mine, other in sources:

            @pl.when(flag)
            def _(k=k, mine=mine, other=other, sems=sems):
                for j in range(parts):
                    pltpu.make_async_copy(mine[j], x.at[k, 0, j], sems[j]).start()
                pltpu.make_async_copy(other, x.at[k, 1], sems[parts]).start()

        chosen.append(
            [pltpu.make_async_copy(own.at[j], x.at[k, 0, j], sems[j]) for j in range(parts)]
            + [pltpu.make_async_copy(own_o, x.at[k, 1], sems[parts])]
        )
    panel_o = loads.start(lc_o, co)
    for k in range(children):
        wait(chosen[k])
        for j in range(parts):
            rows = pl.ds(j * width, width)
            w = lc[k, pl.ds(width + j * width, width), :].astype(F32)
            part = dot(x[k, 0, j, head, :], lc[k, ends[0], :])
            part += dot(x[k, 1, j, head, :], lc[k, ends[1], :])
            v[k, rows, :] = (part - jnp.where(keep_ref[k, j] > 0, w, 0.0)).astype(BF16)
    for k in range(children):
        t[k] = dot(a[...], v[k]).astype(BF16)
    for k in range(children):
        for i in range(2):
            y = dot(x[k, 0, holds[i], tail, :], lc[k, ends[0], :])
            y += dot(x[k, 1, holds[i], tail, :], lc[k, ends[1], :])
            for j in range(parts):
                y += dot_t(x[k, i, j, head, :], t[k, j * width : (j + 1) * width, :])
            cc[k, ends[i], :] = (-y).astype(BF16)
        outs.append(loads.start(cc.at[k], cc_out.at[k, head]))
        for j in range(parts):

            @pl.when(keep_ref[k, j] == 0)
            def _(k=k, j=j):
                t[k, pl.ds(j * width, width), :] = jnp.zeros((width, half), BF16)

        outs.append(loads.start(t.at[k], cc_out.at[k, below]))
    panel_o.wait()
    for k in range(children):
        for i, r in enumerate((lc, co)):
            y = dot_t(r[k, below, :], t[k]) + dot_t(r[k, head, :], cc[k])
            cd[k, ends[i], :] = (dc[k, ends[i], :].astype(F32) - y).astype(BF16)
            outs.append(loads.start(cd.at[k, ends[i]], cd_out.at[k, ends[i]]))
    wait(outs)


def local(ainv_top, l_parent, dinv_parent, keep_parent, l_child, dinv_child, keep_child, parent_of):
    devices = lax.axis_size("row")
    planes = devices // 2
    row = lax.axis_index("row")
    swap = [(i, i ^ 1) for i in range(devices)]
    onward = [(i, i - 2 if i % 2 else i + 2) for i in range(devices)]
    onward = [(i, j) for i, j in onward if 0 <= j < devices]
    cores = [(0, 1), (1, 0)]
    half = l_parent.shape[2]
    width = 2 * half
    tops = l_parent.shape[1]
    parts = tops // width
    rows = width + width // parts
    children = l_child.shape[0]
    direct = planes <= DIRECT
    smem = pl.BlockSpec(memory_space=pltpu.SMEM)
    vmem = pl.BlockSpec(memory_space=pltpu.VMEM)
    hbm = pl.BlockSpec(memory_space=pl.ANY)
    packed = jax.ShapeDtypeStruct((rows, half), BF16)
    *own, whole = pl.pallas_call(
        pack_kernel,
        out_shape=(packed,) * parts + (jax.ShapeDtypeStruct((parts, rows, half), BF16),),
        in_specs=[smem] + [pl.BlockSpec(memory_space=pltpu.HBM)] * 2,
        out_specs=(hbm,) * (parts + 1),
        scratch_shapes=[
            pltpu.VMEM((parts, rows, half), BF16),
            pltpu.SemaphoreType.DMA((3 * parts + 1,)),
        ],
        compiler_params=pltpu.CompilerParams(vmem_limit_bytes=60 << 20),
    )(keep_parent, l_parent[0], dinv_parent[0])
    ainv_top, *own = lax.optimization_barrier((ainv_top, *own))
    got = {"own": whole, "c": l_child, "a": ainv_top}
    got.update((f"own {j}", own[j]) for j in range(parts))

    moves = {}
    for j in range(parts):
        moves[f"swapped {j}"] = (f"own {j}", "row", swap)
        moves[f"beyond {j}"] = (f"swapped {j}", "row", onward)
    for name in ("own", "c", "swapped", "beyond"):
        moves[name + " other"] = (name, "col", cores)
    if direct:
        for k in range(1, planes):
            moves[f"a {k}"] = ("a", "row", [(i, (i + 2 * k) % devices) for i in range(devices)])
        moves["far"] = ("sides", "row", swap)
        moves["near other"] = ("near", "col", cores)
        moves["far other"] = ("far", "col", cores)

    def value(name):
        if name in got:
            return got[name]
        if name in ("swapped", "beyond"):
            got[name] = jnp.stack([value(f"{name} {j}") for j in range(parts)])
        elif name in ("near", "sides"):
            near = jnp.stack([got["a"], *(value(f"a {k}") for k in range(1, planes))])
            sides = near.reshape(planes, near.shape[1], planes, 2, -1)
            sides = jnp.where(row % 2 == 0, sides[:, :, :, 0], sides[:, :, :, 1])
            got["near"] = near
            got["sides"] = sides.reshape(planes, near.shape[1], -1)
        else:
            source, axis, pairs = moves[name]
            got[name] = lax.ppermute(value(source), axis, pairs)
        return got[name]

    for window, sequence in SEQUENCES:
        sequence = [name for name in sequence if name in moves]
        for i, name in enumerate(sequence):
            if name in got:
                continue
            source, axis, pairs = moves[name]
            sent = value(source)
            if i >= window:
                sent = lax.optimization_barrier((sent, value(sequence[i - window])))[0]
            got[name] = lax.ppermute(sent, axis, pairs)
    if direct:
        top = [value(name) for name in ("near", "near other", "far", "far other")]
    else:
        top = [lax.all_gather(ainv_top, ("row", "col"), axis=0, tiled=True)]
    parent_diag, full = pl.pallas_call(
        functools.partial(parent_kernel, direct=direct),
        out_shape=(
            jax.ShapeDtypeStruct((width, half), BF16),
            jax.ShapeDtypeStruct((tops, tops), BF16),
        ),
        in_specs=[hbm] * len(top) + [vmem] * 3,
        out_specs=(vmem,) * 2,
        scratch_shapes=[
            pltpu.VMEM((2, *top[-1].shape) if direct else (16, half), BF16),
            pltpu.VMEM((tops, half), BF16),
            pltpu.SemaphoreType.DMA((4 * devices if direct else 1,)),
        ],
        compiler_params=pltpu.CompilerParams(vmem_limit_bytes=12 << 20),
        cost_estimate=pl.CostEstimate(
            flops=2 * tops * half * (tops + width), bytes_accessed=8 << 20, transcendentals=0
        ),
    )(*top, whole, value("own other"), dinv_parent[0])
    sent = [value(f"{name} {j}") for name in ("swapped", "beyond") for j in range(parts)]
    sent += [value("swapped other"), value("beyond other")]
    child_column, child_diag = pl.pallas_call(
        child_kernel,
        out_shape=(
            jax.ShapeDtypeStruct(l_child.shape, BF16),
            jax.ShapeDtypeStruct(dinv_child.shape, BF16),
        ),
        in_specs=[smem] * 2 + [vmem] * 2 + [hbm, vmem] + [hbm] * (len(sent) + 2),
        out_specs=(hbm,) * 2,
        scratch_shapes=[
            pltpu.VMEM((children, 2, parts, rows, half), BF16),
            pltpu.VMEM(l_child.shape, BF16),
            pltpu.VMEM((children, tops, half), BF16),
            pltpu.VMEM((children, tops, half), BF16),
            pltpu.VMEM((children, width, half), BF16),
            pltpu.VMEM((children, width, half), BF16),
            pltpu.SemaphoreType.DMA((24,)),
        ],
        compiler_params=pltpu.CompilerParams(vmem_limit_bytes=20 << 20),
    )(
        parent_of, keep_child, full, l_child, value("c other"), dinv_child,
        whole, value("own other"), *sent,
    )
    return parent_diag[None], child_column, child_diag


def solution(mesh):
    blocks = P(("poles", "row"), None, "col")
    placed = (
        P(("poles", "row", "col"), None),
        blocks,
        blocks,
        P(("poles", "row"), None),
        blocks,
        blocks,
        P(("poles", "row"), None),
        P(("poles", "row")),
    )
    return jax.shard_map(
        local, mesh=mesh, in_specs=placed, out_specs=(blocks,) * 3, check_vma=False
    )
```
